512 devices in a mesh: rx: 32 (over z, y_lo, core), freq: 16 (over y_hi, x).
Axes of the slice: x: 4, y: 8 (y_hi: 4, y_lo: 2; y = y_hi * 2 + y_lo), z: 8, core: 2. Of those that a mesh axis runs over, the one named last changes fastest.
Arguments:
- spectra: bfloat16 [2, 128, 32, 8192], P(None, 'freq', None, 'rx'), may hold values from -60 to 60
- source_block: int32 [1], replicated, may hold values from 0 to 31
Outputs:
- correlations: bfloat16 [256, 256, 8192], P(None, 'freq', 'rx')
The draws below stay inside these ranges and needn't reach their ends.
All inputs are finite; a program needn't handle non-finite values.
Results may differ from the reference program's by a relative error of at most 0.0057.
Values may be sent and summed in bfloat16 or wider, within the bound.
A program may use at most 64 MiB of HBM per device.

```python
import math
import jax
import jax.numpy as jnp
from jax import lax

F = 128
SRC = 256
W = 32
LAGS = 256
C = 8192
N_RX = 32


def draw_spectra(key, part):
    keys = jax.random.split(key, 3)
    noise = jax.random.normal(keys[0], (2, F, W, C), jnp.float32)
    common = jax.random.normal(keys[1], (2, F, W, 1), jnp.float32)
    coupling = jnp.exp(jax.random.uniform(keys[2], (F, 1, C), jnp.float32, -1.0, 1.0))
    channel = jnp.arange(C, dtype=jnp.float32)
    bins = jnp.arange(F, dtype=jnp.float32)
    delay = channel * (0.375 * LAGS / C)
    angle = -2.0 * math.pi / LAGS * bins[:, None, None] * delay[None, None, :]
    cosine = jnp.cos(angle)
    sine = jnp.sin(angle)
    real_part = coupling * (common[0] * cosine - common[1] * sine)
    imag_part = coupling * (common[0] * sine + common[1] * cosine)
    values = noise + jnp.stack([real_part, imag_part])
    return jnp.clip(values, -60.0, 60.0).astype(jnp.bfloat16)


def setup_inputs(seed: int = 0) -> dict:
    streams_of = jax.random.split(jax.random.key(seed), 3)
    return {
        "spectra": draw_spectra(jax.random.fold_in(streams_of[2], 71), 0),
        "source_block": jax.random.randint(streams_of[1], (1,), 0, N_RX).astype(jnp.int32),
    }


def whiten(planes_in):
    planes = planes_in.astype(jnp.float32)
    magnitude = jnp.sqrt(planes[0] * planes[0] + planes[1] * planes[1])
    padded = jnp.pad(magnitude, ((1, 1), (0, 0), (0, 0)))
    smooth = (padded[:-2] + padded[1:-1] + padded[2:]) / 3.0
    divisor = jnp.maximum(smooth, 0.5)
    return (planes / divisor[None]).astype(jnp.bfloat16)

def build_lag_basis():
    bins = jnp.arange(F, dtype=jnp.int32)
    lagged = jnp.arange(LAGS, dtype=jnp.int32)
    phase = bins[:, None] * lagged[None, :] % LAGS
    angle = phase.astype(jnp.float32) * (2.0 * math.pi / LAGS)
    return jnp.concatenate([jnp.cos(angle), -jnp.sin(angle)], axis=0).astype(jnp.bfloat16)

def reference(spectra, source_block):
    start = (source_block[0] * SRC).astype(jnp.int32)
    source = whiten(lax.dynamic_slice_in_dim(spectra, start, SRC, 3))
    joined_sources = jnp.concatenate([source[0], source[1]], axis=1).astype(jnp.float32)
    basis_table = build_lag_basis().astype(jnp.float32)
    receivers = jnp.moveaxis(spectra.reshape(2, F, W, N_RX, SRC), 3, 0)

    def one_group(group):
        white = whiten(group)
        leading_operand = jnp.concatenate([white[0], white[1]], axis=1).astype(jnp.float32)
        trailing_operand = jnp.concatenate([white[1], -white[0]], axis=1).astype(jnp.float32)
        real_total = jnp.einsum('pgo,pgd->pod', joined_sources, leading_operand)
        imaginary_total = jnp.einsum('pgo,pgd->pod', joined_sources, trailing_operand)
        cross = (jnp.stack([real_total, imaginary_total]) / W).astype(jnp.bfloat16)
        stacked = cross.reshape(2 * F, SRC, SRC).astype(jnp.float32)
        lagged = jnp.einsum('kl,ksr->slr', basis_table, stacked) * (2.0 / F)
        return lagged.astype(jnp.bfloat16)
    groups = lax.map(one_group, receivers)
    return jnp.moveaxis(groups, 0, 2).reshape(SRC, LAGS, C)
```

```python
import functools
import math

import jax
import jax.numpy as jnp
import numpy as np
from jax import lax
from jax.experimental import pallas as pl
from jax.experimental.pallas import tpu as pltpu
from jax.sharding import PartitionSpec as P

F = 128
W = 32
LAGS = 256
NX, NYH, NYL, NZ, NC = 4, 4, 2, 8, 2
NK = NX * NYH
FB = F // NK
LB = LAGS // NK
MESH = pl.DeviceIdType.MESH


def mod(a, n):
    return lax.rem(a + n, n)


def kernel(owner_ref, tw_ref, spec_ref, out_ref, halo, st_own, b1, b1s, b2, sg, rg, rg1, cosb, sinb, lhs, acc,
           halo_send, halo_recv, s1_send, s1_recv, s2_send, s2_recv, sx_send, sx_recv, sy_send, sy_recv,
           z_send, z_recv, c_send, c_recv, ry_send, ry_recv, rx_send, rx_recv):
    r = lax.axis_index("rx")
    k = lax.axis_index("freq")
    z = lax.div(r, 4)
    q = lax.rem(r, 4)
    yl = lax.div(q, 2)
    core = lax.rem(q, 2)
    yh = lax.div(k, 4)
    x = lax.rem(k, 4)

    def dev(z_, yl_, c_, yh_, x_):
        return (z_ * 4 + yl_ * 2 + c_, yh_ * 4 + x_)

    def remote(src, dst, send, recv, device):
        copy = pltpu.make_async_remote_copy(src, dst, send, recv, device_id=device, device_id_type=MESH)
        copy.start()
        return copy

    halo_peers = [(r, mod(k + 1, NK)), (r, mod(k - 1, NK))]
    q_peers = [(z * 4 + lax.rem(q + d, 4), k) for d in range(1, 4)]
    z_peers = [(lax.rem(z + d, NZ) * 4 + q, k) for d in range(1, NZ)]
    x_peers = [dev(z, yl, core, yh, lax.rem(x + d, NX)) for d in range(1, NX)]
    y = yh * 2 + yl
    y_peers = []
    for d in range(1, 8):
        yy = lax.rem(y + d, 8)
        y_peers.append(dev(z, lax.rem(yy, 2), core, lax.div(yy, 2), x))
    everyone = halo_peers + q_peers + z_peers + x_peers + y_peers

    barrier = pltpu.get_barrier_semaphore()
    for peer in everyone:
        pl.semaphore_signal(barrier, inc=1, device_id=peer, device_id_type=MESH)
    pl.semaphore_wait(barrier, len(everyone))

    up, down = halo_peers
    h0 = remote(spec_ref.at[:, FB - 1], halo.at[0], halo_send.at[0], halo_recv.at[0], up)
    h1 = remote(spec_ref.at[:, 0], halo.at[1], halo_send.at[1], halo_recv.at[1], down)

    lane = lax.broadcasted_iota(jnp.int32, (8, FB * W), 1)
    lag = lax.broadcasted_iota(jnp.int32, (8, FB * W), 0) + k * LB

    @pl.loop(0, NK)
    def _(kk):
        bins = kk * FB + lax.shift_right_logical(lane, 5)
        angle = jnp.bitwise_and(bins * lag, LAGS - 1).astype(jnp.float32) * (2.0 * math.pi / LAGS)
        cosb[kk] = jnp.cos(angle)
        sinb[kk] = jnp.sin(angle)

    h0.wait()
    h1.wait()

    def magnitude(a, b):
        return jnp.sqrt(a * a + b * b)

    lower = halo[0].astype(jnp.float32)
    upper = halo[1].astype(jnp.float32)
    m_low = jnp.where(k == 0, 0.0, magnitude(lower[0], lower[1]))
    m_high = jnp.where(k == NK - 1, 0.0, magnitude(upper[0], upper[1]))

    def raw(p, f):
        return spec_ref[p, f].astype(jnp.float32)

    mags = [m_low] + [magnitude(raw(0, f), raw(1, f)) for f in range(FB)] + [m_high]
    for f in range(FB):
        divisor = jnp.maximum((mags[f] + mags[f + 1] + mags[f + 2]) / 3.0, 0.5)
        for p in range(2):
            rg[k, pl.ds(p * 256 + f * W, W), :] = (raw(p, f) / divisor).astype(jnp.bfloat16)

    sends = []

    def ry(slot, block, rows, device):
        view = rg.at[block, rows]
        return remote(view, view, ry_send.at[slot], ry_recv.at[slot], device)

    def rx(row, slot, block, rows, device):
        view = rg.at[block, rows]
        return remote(view, view, rx_send.at[row, slot], rx_recv.at[row, slot], device)

    every = pl.ds(0, 512)
    first, second = pl.ds(0, 256), pl.ds(256, 256)
    y_up = dev(z, yl, core, mod(yh + 1, NYH), x)
    y_dn = dev(z, yl, core, mod(yh - 1, NYH), x)
    x_up = dev(z, yl, core, yh, mod(x + 1, NX))
    x_dn = dev(z, yl, core, yh, mod(x - 1, NX))

    def block_of(dyh, dx):
        return mod(yh + dyh, NYH) * NX + mod(x + dx, NX)

    for p in range(2):
        t = rg[k, pl.ds(p * 256, 256), :].astype(jnp.float32).T.reshape(NZ, 4, 8, FB * W)
        for j in range(4):
            st_own[j, :, pl.ds(p * 8, 8), :] = t[:, j].astype(jnp.bfloat16)
    s1 = [remote(st_own.at[lax.rem(q + d, 4)], b1.at[q], s1_send.at[d], s1_recv.at[d], q_peers[d - 1])
          for d in range(1, 4)]
    y_own = [ry(0, k, every, y_up), ry(1, k, every, y_dn)]
    x_own = [rx(0, 0, k, every, x_up), rx(0, 1, k, every, x_dn)]
    b1[q] = st_own[q]
    for c in s1:
        c.wait()
    owner = owner_ref[0]
    b1s[...] = b1[lax.rem(owner, 4)]
    s2 = [remote(b1s.at[lax.rem(z + d, NZ)], b2.at[z], s2_send.at[d], s2_recv.at[d], z_peers[d - 1])
          for d in range(1, NZ)]
    b2[z] = b1s[z]
    for c in s2:
        c.wait()
    sg[z, core, yl, k] = b2[lax.div(owner, 4)]
    mine = sg.at[z, core, yl, k]
    sx = [remote(mine, mine, sx_send.at[d], sx_recv.at[d], x_peers[d - 1]) for d in range(1, NX)]
    for c in sx:
        c.wait()
    row = sg.at[z, core, yl, pl.ds(yh * NX, NX)]
    sy = [remote(row, row, sy_send.at[d], sy_recv.at[d], y_peers[d - 1]) for d in range(1, 8)]
    for c in sy:
        c.wait()

    z_up = dev(mod(z + 1, NZ), yl, core, yh, x)
    z_dn = dev(mod(z - 1, NZ), yl, core, yh, x)
    sibling = dev(z, yl, 1 - core, yh, x)

    def zstep(t):
        a = sg.at[mod(z - t, NZ), core]
        b = sg.at[mod(z + t, NZ), core]
        if t == 3:
            a, b = a.at[0], b.at[1]
        return [remote(a, a, z_send.at[0, t], z_recv.at[0, t], z_up),
                remote(b, b, z_send.at[1, t], z_recv.at[1, t], z_dn)]

    def share(slot, zz):
        view = sg.at[zz, core]
        return remote(view, view, c_send.at[slot], c_recv.at[slot], sibling)

    zs = zstep(0)
    cs = [share(0, z)]

    for c in y_own:
        c.wait_recv()
    sends += y_own
    y_far = [ry(2, block_of(-1, 0), first, y_up), ry(3, block_of(1, 0), second, y_dn)]
    x_next = [[rx(1, 0, block_of(-1, 0), every, x_up), rx(1, 1, block_of(-1, 0), every, x_dn)],
              [rx(2, 0, block_of(1, 0), every, x_up), rx(2, 1, block_of(1, 0), every, x_dn)]]
    for c in x_own:
        c.wait_recv()
    sends += x_own
    fars = [[rx(0, 2, block_of(0, -1), first, x_up), rx(0, 3, block_of(0, 1), second, x_dn)]]
    for c in zs:
        c.wait_recv()
    sends += zs
    zs = zstep(1)
    cs += [share(1, mod(z - 1, NZ)), share(2, mod(z + 1, NZ))]
    for c in y_far:
        c.wait_recv()
    sends += y_far
    x_next.append([rx(3, 0, block_of(2, 0), every, x_up), rx(3, 1, block_of(2, 0), every, x_dn)])
    for c in zs:
        c.wait_recv()
    sends += zs
    zs = zstep(2)
    cs += [share(3, mod(z - 2, NZ)), share(4, mod(z + 2, NZ))]
    for i, dy in ((1, -1), (2, 1), (3, 2)):
        for c in x_next[i - 1]:
            c.wait_recv()
        sends += x_next[i - 1]
        fars.append([rx(i, 2, block_of(dy, -1), first, x_up), rx(i, 3, block_of(dy, 1), second, x_dn)])
        if i == 1:
            for c in zs:
                c.wait_recv()
            sends += zs
            zs = zstep(3)
            cs += [share(5, mod(z - 3, NZ)), share(6, mod(z + 3, NZ))]
    for c in zs:
        c.wait_recv()
    sends += zs
    cs += [share(7, mod(z + 4, NZ))]
    for pair in fars:
        for c in pair:
            c.wait_recv()
        sends += pair
    for c in cs:
        c.wait()
    for c in sends:
        c.wait_send()

    acc[...] = jnp.zeros_like(acc)

    @pl.loop(0, NK)
    def _(kk):
        phase = lax.rem(kk, 4) * FB
        for f in range(FB):
            a = rg[kk, pl.ds(f * W, W), :].astype(jnp.float32)
            b = rg[kk, pl.ds(256 + f * W, W), :].astype(jnp.float32)
            cr, ci = tw_ref[phase + f], tw_ref[32 + phase + f]
            rg1[pl.ds(f * W, W), :] = (a * cr - b * ci).astype(jnp.bfloat16)
            rg1[pl.ds(256 + f * W, W), :] = (b * cr + a * ci).astype(jnp.bfloat16)

        @pl.loop(0, NZ)
        def _(zz):
            co, si = cosb[kk][None], sinb[kk][None]
            for j in range(4):
                chunk = sg[zz, j % 2, j // 2, kk].astype(jnp.float32)
                s0, s1_ = chunk[:8][:, None, :], chunk[8:][:, None, :]
                rows = pl.ds(j * 64, 64)
                lhs[rows, pl.ds(0, 256)] = (co * s0 + si * s1_).reshape(64, 256).astype(jnp.bfloat16)
                lhs[rows, pl.ds(256, 256)] = (co * s1_ - si * s0).reshape(64, 256).astype(jnp.bfloat16)
            left = lhs[...]
            acc[zz, 0] += jnp.dot(left, rg[kk], preferred_element_type=jnp.float32)
            acc[zz, 1] += jnp.dot(left, rg1[...], preferred_element_type=jnp.float32)

    @pl.loop(0, NZ)
    def _(zz):
        low = acc[zz, 0].reshape(32, 8, 256)
        high = acc[zz, 1].reshape(32, 8, 256)
        both = jnp.concatenate([low, high], axis=1) * (2.0 / F / W)
        out_ref[pl.ds(zz * 32, 32)] = both.astype(jnp.bfloat16)


def on_device(spectra, source_block):
    angles = np.arange(32) * (2.0 * math.pi / 32)
    table = jnp.asarray(np.concatenate([np.cos(angles), np.sin(angles)]).astype(np.float32))
    dma = pltpu.SemaphoreType.DMA
    bf = jnp.bfloat16
    return pl.pallas_call(
        kernel,
        out_shape=jax.ShapeDtypeStruct((256, LB, 256), bf),
        in_specs=[
            pl.BlockSpec(memory_space=pltpu.SMEM),
            pl.BlockSpec(memory_space=pltpu.SMEM),
            pl.BlockSpec(memory_space=pltpu.VMEM),
        ],
        out_specs=pl.BlockSpec(memory_space=pltpu.VMEM),
        scratch_shapes=[
            pltpu.VMEM((2, 2, W, 256), bf),
            pltpu.VMEM((4, NZ, 16, 256), bf),
            pltpu.VMEM((4, NZ, 16, 256), bf),
            pltpu.VMEM((NZ, 16, 256), bf),
            pltpu.VMEM((NZ, 16, 256), bf),
            pltpu.VMEM((NZ, NC, NYL, NK, 16, 256), bf),
            pltpu.VMEM((NK, 512, 256), bf),
            pltpu.VMEM((512, 256), bf),
            pltpu.VMEM((NK, 8, 256), jnp.float32),
            pltpu.VMEM((NK, 8, 256), jnp.float32),
            pltpu.VMEM((256, 512), bf),
            pltpu.VMEM((NZ, 2, 256, 256), jnp.float32),
            dma((2,)), dma((2,)),
            dma((4,)), dma((4,)),
            dma((8,)), dma((8,)),
            dma((4,)), dma((4,)),
            dma((8,)), dma((8,)),
            dma((2, 4)), dma((2, 4)),
            dma((8,)), dma((8,)),
            dma((4,)), dma((4,)),
            dma((4, 4)), dma((4, 4)),
        ],
        compiler_params=pltpu.CompilerParams(
            collective_id=0, has_side_effects=True, vmem_limit_bytes=40 * 2**20
        ),
        cost_estimate=pl.CostEstimate(flops=2 * 4096 * 8192 * 256, bytes_accessed=3 * 2**20, transcendentals=0),
    )(source_block, table, spectra)


def solution(mesh):
    in_specs = (P(None, "freq", None, "rx"), P())
    out_specs = P(None, "freq", "rx")
    return jax.shard_map(
        on_device, mesh=mesh, in_specs=in_specs, out_specs=out_specs, check_vma=False
    )
```

```python
import functools
import math

import jax
import jax.numpy as jnp
import numpy as np
from jax import lax
from jax.experimental import pallas as pl
from jax.experimental.pallas import tpu as pltpu
from jax.sharding import PartitionSpec as P

F = 128
W = 32
LAGS = 256
NX, NYH, NYL, NZ, NC = 4, 4, 2, 8, 2
NK = NX * NYH
FB = F // NK
LB = LAGS // NK
MESH = pl.DeviceIdType.MESH


def mod(a, n):
    return lax.rem(a + n, n)


def kernel(owner_ref, tw_ref, spec_ref, out_ref, halo, st_own, b1, b1s, b2, sg, rg, rg1, cosb, sinb, lhs, acc,
           halo_send, halo_recv, s1_send, s1_recv, s2_send, s2_recv, sx_send, sx_recv, sy_send, sy_recv,
           z_send, z_recv, c_send, c_recv, ry_send, ry_recv, rx_send, rx_recv):
    r = lax.axis_index("rx")
    k = lax.axis_index("freq")
    z = lax.div(r, 4)
    q = lax.rem(r, 4)
    yl = lax.div(q, 2)
    core = lax.rem(q, 2)
    yh = lax.div(k, 4)
    x = lax.rem(k, 4)

    def dev(z_, yl_, c_, yh_, x_):
        return (z_ * 4 + yl_ * 2 + c_, yh_ * 4 + x_)

    def remote(src, dst, send, recv, device):
        copy = pltpu.make_async_remote_copy(src, dst, send, recv, device_id=device, device_id_type=MESH)
        copy.start()
        return copy

    halo_peers = [(r, mod(k + 1, NK)), (r, mod(k - 1, NK))]
    q_peers = [(z * 4 + lax.rem(q + d, 4), k) for d in range(1, 4)]
    z_peers = [(lax.rem(z + d, NZ) * 4 + q, k) for d in range(1, NZ)]
    x_peers = [dev(z, yl, core, yh, lax.rem(x + d, NX)) for d in range(1, NX)]
    y = yh * 2 + yl
    y_peers = []
    for d in range(1, 8):
        yy = lax.rem(y + d, 8)
        y_peers.append(dev(z, lax.rem(yy, 2), core, lax.div(yy, 2), x))
    everyone = halo_peers + q_peers + z_peers + x_peers + y_peers

    barrier = pltpu.get_barrier_semaphore()
    for peer in everyone:
        pl.semaphore_signal(barrier, inc=1, device_id=peer, device_id_type=MESH)
    pl.semaphore_wait(barrier, len(everyone))

    up, down = halo_peers
    h0 = remote(spec_ref.at[:, FB - 1], halo.at[0], halo_send.at[0], halo_recv.at[0], up)
    h1 = remote(spec_ref.at[:, 0], halo.at[1], halo_send.at[1], halo_recv.at[1], down)

    lane = lax.broadcasted_iota(jnp.int32, (8, FB * W), 1)
    lag = lax.broadcasted_iota(jnp.int32, (8, FB * W), 0) + k * LB

    @pl.loop(0, NK)
    def _(kk):
        bins = kk * FB + lax.shift_right_logical(lane, 5)
        angle = jnp.bitwise_and(bins * lag, LAGS - 1).astype(jnp.float32) * (2.0 * math.pi / LAGS)
        cosb[kk] = jnp.cos(angle)
        sinb[kk] = jnp.sin(angle)

    h0.wait()
    h1.wait()

    def magnitude(a, b):
        return jnp.sqrt(a * a + b * b)

    lower = halo[0].astype(jnp.float32)
    upper = halo[1].astype(jnp.float32)
    m_low = jnp.where(k == 0, 0.0, magnitude(lower[0], lower[1]))
    m_high = jnp.where(k == NK - 1, 0.0, magnitude(upper[0], upper[1]))

    def raw(p, f):
        return spec_ref[p, f].astype(jnp.float32)

    mags = [m_low] + [magnitude(raw(0, f), raw(1, f)) for f in range(FB)] + [m_high]
    for f in range(FB):
        divisor = jnp.maximum((mags[f] + mags[f + 1] + mags[f + 2]) / 3.0, 0.5)
        for p in range(2):
            rg[k, pl.ds(p * 256 + f * W, W), :] = (raw(p, f) / divisor).astype(jnp.bfloat16)

    half = (pl.ds(0, 256), pl.ds(256, 256))
    y_to = (dev(z, yl, core, mod(yh + 1, NYH), x), dev(z, yl, core, mod(yh - 1, NYH), x))
    x_to = (dev(z, yl, core, yh, mod(x + 1, NX)), dev(z, yl, core, yh, mod(x - 1, NX)))
    sibling = dev(z, yl, 1 - core, yh, x)
    sends = []

    ring = jnp.where(core == 0, z, y)
    other = jnp.where(core == 0, y, z)

    def on_ring(a, b):
        zz, yy = jnp.where(core == 0, a, b), jnp.where(core == 0, b, a)
        return dev(zz, lax.rem(yy, 2), core, lax.div(yy, 2), x)

    ring_to = (on_ring(mod(ring + 1, 8), other), on_ring(mod(ring - 1, 8), other))

    def block_of(dyh, dx):
        return mod(yh + dyh, NYH) * NX + mod(x + dx, NX)

    def ry(way, slot, block, h):
        view = rg.at[block, half[h]]
        c = remote(view, view, ry_send.at[way, slot], ry_recv.at[way, slot], y_to[way])
        sends.append(c)
        return c

    def rx(row, way, slot, block, h):
        view = rg.at[block, half[h]]
        c = remote(view, view, rx_send.at[row, way, slot], rx_recv.at[row, way, slot], x_to[way])
        sends.append(c)
        return c

    def got(*copies):
        for c in copies:
            c.wait_recv()

    def xsend(row, block, h):
        return {(0, h): rx(row, 0, h, block, h), (1, h): rx(row, 1, h, block, h)}

    def rstep(t, u):
        pair = []
        for way in range(2):
            if t < 3 or way == u:
                view = sg.at[core, mod(ring - t, 8) if way == 0 else mod(ring + t, 8), pl.ds(u * 4, 4)]
                pair.append(remote(view, view, z_send.at[way, t, u], z_recv.at[way, t, u], ring_to[way]))
        sends.extend(pair)
        return pair

    cs = []

    def share(slot, a):
        view = sg.at[core, mod(ring + a, 8)]
        cs.append(remote(view, view, c_send.at[slot], c_recv.at[slot], sibling))

    for p in range(2):
        t = rg[k, pl.ds(p * 256, 256), :].astype(jnp.float32).T.reshape(NZ, 4, 8, FB * W)
        for j in range(4):
            st_own[j, :, pl.ds(p * 8, 8), :] = t[:, j].astype(jnp.bfloat16)
    s1 = [remote(st_own.at[lax.rem(q + d, 4)], b1.at[q], s1_send.at[d], s1_recv.at[d], q_peers[d - 1])
          for d in range(1, 4)]
    y0 = (ry(0, 0, k, 0), ry(1, 1, k, 1))
    x0 = {(0, 0): rx(0, 0, 0, k, 0), (1, 1): rx(0, 1, 1, k, 1)}
    y1 = (ry(0, 1, k, 1), ry(1, 0, k, 0))
    x0[0, 1] = rx(0, 0, 1, k, 1)
    x0[1, 0] = rx(0, 1, 0, k, 0)
    b1[q] = st_own[q]
    for c in s1:
        c.wait()
    owner = owner_ref[0]
    b1s[...] = b1[lax.rem(owner, 4)]
    s2 = [remote(b1s.at[lax.rem(z + d, NZ)], b2.at[z], s2_send.at[d], s2_recv.at[d], z_peers[d - 1])
          for d in range(1, NZ)]
    b2[z] = b1s[z]
    got(x0[0, 0], x0[1, 1])
    f0 = (rx(0, 0, 2, block_of(0, -1), 0), rx(0, 1, 2, block_of(0, 1), 1))
    for c in s2:
        c.wait()
    sg[core, ring, other, x] = b2[lax.div(owner, 4)]
    mine = sg.at[core, ring, other, x]
    sx = [remote(mine, mine, sx_send.at[d], sx_recv.at[d], x_peers[d - 1]) for d in range(1, NX)]
    got(*y0)
    y2 = (ry(0, 2, block_of(-1, 0), 0), ry(1, 2, block_of(1, 0), 1))
    x1 = xsend(1, block_of(-1, 0), 0)
    x2 = xsend(2, block_of(1, 0), 1)
    for c in sx:
        c.wait()
    srow = sg.at[core, ring, other]
    sy = [remote(srow, srow, sy_send.at[d], sy_recv.at[d], on_ring(ring, lax.rem(other + d, 8)))
          for d in range(1, 8)]
    got(*y1)
    x1.update(xsend(1, block_of(-1, 0), 1))
    x2.update(xsend(2, block_of(1, 0), 0))
    for c in sy:
        c.wait()
    ra, rb = rstep(0, 0), rstep(0, 1)
    share(0, 0)
    got(x1[0, 0], x2[1, 1])
    f1 = [rx(1, 0, 2, block_of(-1, -1), 0)]
    f2 = [rx(2, 1, 2, block_of(1, 1), 1)]
    got(*y2)
    x3 = xsend(3, block_of(2, 0), 0)
    x3.update(xsend(3, block_of(2, 0), 1))
    for t in range(1, 4):
        got(*ra)
        ra = rstep(t, 0)
        got(*rb)
        rb = rstep(t, 1)
        share(2 * t - 1, -t)
        share(2 * t, t)
        if t == 1:
            got(x1[1, 1], x2[0, 0])
            f1.append(rx(1, 1, 2, block_of(-1, 1), 1))
            f2.append(rx(2, 0, 2, block_of(1, -1), 0))
    got(*ra, *rb)
    share(7, 4)
    got(x3[0, 0], x3[1, 1])
    f3 = [rx(3, 0, 2, block_of(2, -1), 0), rx(3, 1, 2, block_of(2, 1), 1)]
    for c in cs:
        c.wait()
    def last():
        for c in sends:
            c.wait_send()

    def process(dy):
        row = mod(yh + dy, NYH)

        @pl.loop(0, 2)
        def _(pair):
            for i in range(2):
                xx = pair * 2 + i
                kk = row * NX + xx
                for f in range(FB):
                    a = rg[kk, pl.ds(f * W, W), :].astype(jnp.float32)
                    b = rg[kk, pl.ds(256 + f * W, W), :].astype(jnp.float32)
                    phase = lax.rem(kk, 4) * FB + f
                    cr, ci = tw_ref[phase], tw_ref[32 + phase]
                    rg1[pl.ds(i * 512 + f * W, W), :] = (a * cr - b * ci).astype(jnp.bfloat16)
                    rg1[pl.ds(i * 512 + 256 + f * W, W), :] = (b * cr + a * ci).astype(jnp.bfloat16)

                @pl.loop(0, NZ)
                def _(zz):
                    co, si = cosb[kk][None], sinb[kk][None]
                    for yl_ in range(2):
                        for c_ in range(2):
                            yy = row * 2 + yl_
                            chunk = (sg[0, zz, yy, xx] if c_ == 0 else sg[1, yy, zz, xx]).astype(jnp.float32)
                            s0, s1_ = chunk[:8][:, None, :], chunk[8:][:, None, :]
                            rows = pl.ds((yl_ * 2 + c_) * 64, 64)
                            lhs[zz, rows, pl.ds(i * 512, 256)] = (
                                (co * s0 + si * s1_).reshape(64, 256).astype(jnp.bfloat16))
                            lhs[zz, rows, pl.ds(i * 512 + 256, 256)] = (
                                (co * s1_ - si * s0).reshape(64, 256).astype(jnp.bfloat16))

            left = lhs[...].reshape(2048, 1024)
            right = rg[pl.ds(row * NX + pair * 2, 2)].reshape(1024, 256)
            acc[0] += jnp.dot(left, right, preferred_element_type=jnp.float32)
            acc[1] += jnp.dot(left, rg1[...], preferred_element_type=jnp.float32)

    acc[...] = jnp.zeros_like(acc)
    got(x0[0, 1], x0[1, 0], *f0)
    process(0)
    got(x1[0, 1], x1[1, 0], *f1)
    process(-1)
    got(x2[0, 1], x2[1, 0], *f2)
    process(1)
    got(x3[0, 1], x3[1, 0], *f3)
    process(2)
    last()

    @pl.loop(0, NZ)
    def _(zz):
        rows = pl.ds(zz * 256, 256)
        low = acc[0, rows, :].reshape(32, 8, 256)
        high = acc[1, rows, :].reshape(32, 8, 256)
        both = jnp.concatenate([low, high], axis=1) * (2.0 / F / W)
        out_ref[pl.ds(zz * 32, 32)] = both.astype(jnp.bfloat16)


def on_device(spectra, source_block):
    angles = np.arange(32) * (2.0 * math.pi / 32)
    table = jnp.asarray(np.concatenate([np.cos(angles), np.sin(angles)]).astype(np.float32))
    dma = pltpu.SemaphoreType.DMA
    bf = jnp.bfloat16
    return pl.pallas_call(
        kernel,
        out_shape=jax.ShapeDtypeStruct((256, LB, 256), bf),
        in_specs=[
            pl.BlockSpec(memory_space=pltpu.SMEM),
            pl.BlockSpec(memory_space=pltpu.SMEM),
            pl.BlockSpec(memory_space=pltpu.VMEM),
        ],
        out_specs=pl.BlockSpec(memory_space=pltpu.VMEM),
        scratch_shapes=[
            pltpu.VMEM((2, 2, W, 256), bf),
            pltpu.VMEM((4, NZ, 16, 256), bf),
            pltpu.VMEM((4, NZ, 16, 256), bf),
            pltpu.VMEM((NZ, 16, 256), bf),
            pltpu.VMEM((NZ, 16, 256), bf),
            pltpu.VMEM((NC, 8, 8, NX, 16, 256), bf),
            pltpu.VMEM((NK, 512, 256), bf),
            pltpu.VMEM((1024, 256), bf),
            pltpu.VMEM((NK, 8, 256), jnp.float32),
            pltpu.VMEM((NK, 8, 256), jnp.float32),
            pltpu.VMEM((NZ, 256, 1024), bf),
            pltpu.VMEM((2, 2048, 256), jnp.float32),
            dma((2,)), dma((2,)),
            dma((4,)), dma((4,)),
            dma((8,)), dma((8,)),
            dma((4,)), dma((4,)),
            dma((8,)), dma((8,)),
            dma((2, 4, 2)), dma((2, 4, 2)),
            dma((8,)), dma((8,)),
            dma((2, 3)), dma((2, 3)),
            dma((4, 2, 3)), dma((4, 2, 3)),
        ],
        compiler_params=pltpu.CompilerParams(
            collective_id=0, has_side_effects=True, vmem_limit_bytes=48 * 2**20
        ),
        cost_estimate=pl.CostEstimate(flops=2 * 4096 * 8192 * 256, bytes_accessed=3 * 2**20, transcendentals=0),
    )(source_block, table, spectra)


def solution(mesh):
    in_specs = (P(None, "freq", None, "rx"), P())
    out_specs = P(None, "freq", "rx")
    return jax.shard_map(
        on_device, mesh=mesh, in_specs=in_specs, out_specs=out_specs, check_vma=False
    )
```

```python
import math

import jax
import jax.numpy as jnp
from jax import lax
from jax.experimental import pallas as pl
from jax.experimental.pallas import tpu as pltpu
from jax.sharding import PartitionSpec as P

F = 128
W = 32
LAGS = 256
NX, NYH, NYL, NZ, NC = 4, 4, 2, 8, 2
NK = NX * NYH
FB = F // NK
LB = LAGS // NK
MESH = pl.DeviceIdType.MESH


def mod(a, n):
    return lax.rem(a + n, n)


def kernel(owner_ref, spec_hbm, out_ref, spec_ref, halo, st_own, b1, b1s, b2, sg, rg, rg1, cosb, sinb, lhs, acc, turned,
           spec_sem, halo_send, halo_recv, s1_send, s1_recv, s2_send, s2_recv, sx_send, sx_recv, sy_send, sy_recv,
           z_send, z_recv, c_send, c_recv, ry_send, ry_recv, rx_send, rx_recv):
    r = lax.axis_index("rx")
    k = lax.axis_index("freq")
    z = lax.div(r, 4)
    q = lax.rem(r, 4)
    yl = lax.div(q, 2)
    core = lax.rem(q, 2)
    yh = lax.div(k, 4)
    x = lax.rem(k, 4)

    def dev(z_, yl_, c_, yh_, x_):
        return (z_ * 4 + yl_ * 2 + c_, yh_ * 4 + x_)

    def remote(src, dst, send, recv, device):
        copy = pltpu.make_async_remote_copy(src, dst, send, recv, device_id=device, device_id_type=MESH)
        copy.start()
        return copy

    halo_peers = [(r, mod(k + 1, NK)), (r, mod(k - 1, NK))]
    q_peers = [(z * 4 + lax.rem(q + d, 4), k) for d in range(1, 4)]
    z_peers = [(lax.rem(z + d, NZ) * 4 + q, k) for d in range(1, NZ)]
    x_peers = [dev(z, yl, core, yh, lax.rem(x + d, NX)) for d in range(1, NX)]
    y = yh * 2 + yl
    y_peers = []
    for d in range(1, 8):
        yy = lax.rem(y + d, 8)
        y_peers.append(dev(z, lax.rem(yy, 2), core, lax.div(yy, 2), x))
    everyone = halo_peers + q_peers + z_peers + x_peers + y_peers

    fetch = pltpu.make_async_copy(spec_hbm, spec_ref, spec_sem.at[0])
    fetch.start()
    barrier = pltpu.get_barrier_semaphore()
    for peer in everyone:
        pl.semaphore_signal(barrier, inc=1, device_id=peer, device_id_type=MESH)
    pl.semaphore_wait(barrier, len(everyone))

    up, down = halo_peers
    h0 = remote(spec_hbm.at[:, FB - 1], halo.at[0], halo_send.at[0], halo_recv.at[0], up)
    h1 = remote(spec_hbm.at[:, 0], halo.at[1], halo_send.at[1], halo_recv.at[1], down)

    lane = lax.broadcasted_iota(jnp.int32, (8, FB * W), 1)
    lag = lax.broadcasted_iota(jnp.int32, (8, FB * W), 0) + k * LB

    @pl.loop(0, NK)
    def _(kk):
        bins = kk * FB + lax.shift_right_logical(lane, 5)
        angle = jnp.bitwise_and(bins * lag, LAGS - 1).astype(jnp.float32) * (2.0 * math.pi / LAGS)
        for table, values in ((cosb, jnp.cos(angle)), (sinb, jnp.sin(angle))):
            for c in range(2):
                for lc in range(8):
                    line = values[lc:lc + 1, c * 128:(c + 1) * 128]
                    table[kk, c, lc] = jnp.broadcast_to(line, (16, 128)).astype(jnp.bfloat16)

    fetch.wait()
    acc[...] = jnp.zeros_like(acc)
    h0.wait()
    h1.wait()

    def magnitude(a, b):
        return jnp.sqrt(a * a + b * b)

    lower = halo[0].astype(jnp.float32)
    upper = halo[1].astype(jnp.float32)
    m_low = jnp.where(k == 0, 0.0, magnitude(lower[0], lower[1]))
    m_high = jnp.where(k == NK - 1, 0.0, magnitude(upper[0], upper[1]))

    def raw(p, f):
        return spec_ref[p, f].astype(jnp.float32)

    mags = [m_low] + [magnitude(raw(0, f), raw(1, f)) for f in range(FB)] + [m_high]
    for f in range(FB):
        divisor = jnp.maximum((mags[f] + mags[f + 1] + mags[f + 2]) / 3.0, 0.5)
        for p in range(2):
            rg[k, pl.ds(f // 4 * 256 + p * 128 + f % 4 * W, W), :] = (raw(p, f) / divisor).astype(jnp.bfloat16)

    half = (pl.ds(0, 256), pl.ds(256, 256))
    y_to = (dev(z, yl, core, mod(yh + 1, NYH), x), dev(z, yl, core, mod(yh - 1, NYH), x))
    x_to = (dev(z, yl, core, yh, mod(x + 1, NX)), dev(z, yl, core, yh, mod(x - 1, NX)))
    sibling = dev(z, yl, 1 - core, yh, x)
    sends = []

    ring = jnp.where(core == 0, z, y)
    other = jnp.where(core == 0, y, z)

    def on_ring(a, b):
        zz, yy = jnp.where(core == 0, a, b), jnp.where(core == 0, b, a)
        return dev(zz, lax.rem(yy, 2), core, lax.div(yy, 2), x)

    ring_to = (on_ring(mod(ring + 1, 8), other), on_ring(mod(ring - 1, 8), other))

    def block_of(dyh, dx):
        return mod(yh + dyh, NYH) * NX + mod(x + dx, NX)

    def launch(make):
        make().start()
        sends.append(make)
        return make

    def ry(way, slot, block, h):
        def make():
            view = rg.at[block_of(*block), half[h]]
            return pltpu.make_async_remote_copy(view, view, ry_send.at[way, slot], ry_recv.at[way, slot],
                                                device_id=y_to[way], device_id_type=MESH)

        return launch(make)

    def rx(row, way, slot, block, h):
        def make():
            view = rg.at[block_of(*block), half[h]]
            return pltpu.make_async_remote_copy(view, view, rx_send.at[row, way, slot], rx_recv.at[row, way, slot],
                                                device_id=x_to[way], device_id_type=MESH)

        return launch(make)

    def got(*copies):
        for c in copies:
            (c() if callable(c) else c).wait_recv()

    def xsend(row, block, h):
        return {(0, h): rx(row, 0, h, block, h), (1, h): rx(row, 1, h, block, h)}

    def rpart(t, u, way):
        def make():
            view = sg.at[core, mod(ring - t, 8) if way == 0 else mod(ring + t, 8), pl.ds(u * 4, 4)]
            return pltpu.make_async_remote_copy(view, view, z_send.at[way, t, u], z_recv.at[way, t, u],
                                                device_id=ring_to[way], device_id_type=MESH)

        return launch(make)

    def rstep(t, u):
        return [rpart(t, u, way) for way in range(2) if t < 3 or way == u]

    cs = []

    def share(slot, a):
        def make():
            view = sg.at[core, mod(ring + a, 8)]
            return pltpu.make_async_remote_copy(view, view, c_send.at[slot], c_recv.at[slot],
                                                device_id=sibling, device_id_type=MESH)

        cs.append(launch(make))

    def build(c, a):
        @pl.loop(0, 8)
        def _(b):
            zz, yy = jnp.where(c == 0, a, b), jnp.where(c == 0, b, a)
            row, yl_ = lax.div(yy, 2), lax.rem(yy, 2)
            for xx in range(NX):
                kk = row * NX + xx
                s0, s1_ = sg[c, a, b, xx, 0], sg[c, a, b, xx, 1]
                for lc in range(8):
                    co, si = cosb[kk, c, lc], sinb[kk, c, lc]
                    rows = pl.ds(pl.multiple_of(zz * 256 + lc * 32 + yl_ * 16, 16), 16)
                    lhs[c, row, rows, pl.ds(xx * 256, 128)] = co * s0 + si * s1_
                    lhs[c, row, rows, pl.ds(xx * 256 + 128, 128)] = co * s1_ - si * s0

    def process(c, row):
        for xx in range(NX):
            kk = row * NX + xx
            for g in range(4):
                angles = [2.0 * math.pi / 32 * (xx * FB + m * 4 + g) for m in range(2)]
                cr = jnp.where(c == 0, math.cos(angles[0]), math.cos(angles[1]))
                ci = jnp.where(c == 0, math.sin(angles[0]), math.sin(angles[1]))
                a = rg[kk, pl.ds(pl.multiple_of(c * 256 + g * W, W), W), :].astype(jnp.float32)
                b = rg[kk, pl.ds(pl.multiple_of(c * 256 + 128 + g * W, W), W), :].astype(jnp.float32)
                rg1[pl.ds(xx * 256 + g * W, W), :] = (a * cr - b * ci).astype(jnp.bfloat16)
                rg1[pl.ds(xx * 256 + 128 + g * W, W), :] = (b * cr + a * ci).astype(jnp.bfloat16)
        left = lhs[c, row]
        right = rg[pl.ds(row * NX, NX), pl.ds(pl.multiple_of(c * 256, 256), 256), :].reshape(1024, 256)
        acc[0] += jnp.dot(left, right, preferred_element_type=jnp.float32)
        acc[1] += jnp.dot(left, rg1[...], preferred_element_type=jnp.float32)

    for p in range(2):
        for c in range(2):
            t = rg[k, pl.ds(c * 256 + p * 128, 128), :].astype(jnp.float32).T.astype(jnp.bfloat16)
            t = t.reshape(NZ, 2, 16, 128)
            for yl_ in range(2):
                st_own[yl_ * 2 + c, :, p] = t[:, yl_]
    s1 = [remote(st_own.at[lax.rem(q + d, 4)], b1.at[q], s1_send.at[d], s1_recv.at[d], q_peers[d - 1])
          for d in range(1, 4)]
    T = {}
    plan = dict(y0=0, y1=0, g0=2, y2=3, g1=3, fa=3, fb=4, g2=6, f3=7)

    def at(point):
        for name, step in events:
            if plan[name] == point:
                step()

    def y0():
        T["y0"] = (ry(0, 0, (0, 0), 0), ry(1, 1, (0, 0), 1))

    def y1():
        T["y1"] = (ry(0, 1, (0, 0), 1), ry(1, 0, (0, 0), 0))

    def g0():
        got(*T["y0"])
        T["x1"] = xsend(1, (-1, 0), 0)
        T["x2"] = xsend(2, (1, 0), 1)

    def y2():
        T["y2"] = (ry(0, 2, (-1, 0), 0), ry(1, 2, (1, 0), 1))

    def g1():
        got(*T["y1"])
        T["x1"].update(xsend(1, (-1, 0), 1))
        T["x2"].update(xsend(2, (1, 0), 0))

    def fa():
        got(T["x1"][0, 0], T["x2"][1, 1])
        T["f1"] = [rx(1, 0, 2, (-1, -1), 0)]
        T["f2"] = [rx(2, 1, 2, (1, 1), 1)]

    def fb():
        got(T["x1"][1, 1], T["x2"][0, 0])
        T["f1"].append(rx(1, 1, 2, (-1, 1), 1))
        T["f2"].append(rx(2, 0, 2, (1, -1), 0))

    def g2():
        got(*T["y2"])
        T["x3"] = xsend(3, (2, 0), 0)
        T["x3"].update(xsend(3, (2, 0), 1))

    def f3():
        got(T["x3"][0, 0], T["x3"][1, 1])
        T["f3"] = [rx(3, 0, 2, (2, -1), 0), rx(3, 1, 2, (2, 1), 1)]

    events = [("y0", y0), ("y1", y1), ("g0", g0), ("y2", y2), ("g1", g1), ("fa", fa), ("fb", fb), ("g2", g2), ("f3", f3)]

    at(0)
    x0 = {(0, 0): rx(0, 0, 0, (0, 0), 0), (1, 1): rx(0, 1, 1, (0, 0), 1)}
    x0[0, 1] = rx(0, 0, 1, (0, 0), 1)
    x0[1, 0] = rx(0, 1, 0, (0, 0), 0)
    b1[q] = st_own[q]
    got(*s1)
    sends.extend(s1)
    owner = owner_ref[0]
    b1s[...] = b1[lax.rem(owner, 4)]
    s2 = [remote(b1s.at[lax.rem(z + d, NZ)], b2.at[z], s2_send.at[d], s2_recv.at[d], z_peers[d - 1])
          for d in range(1, NZ)]
    b2[z] = b1s[z]
    at(1)
    got(x0[0, 0], x0[1, 1])
    f0 = (rx(0, 0, 2, (0, -1), 0), rx(0, 1, 2, (0, 1), 1))
    got(*s2)
    sends.extend(s2)
    sg[core, ring, other, x] = b2[lax.div(owner, 4)]
    mine = sg.at[core, ring, other, x]
    sx = [remote(mine, mine, sx_send.at[d], sx_recv.at[d], x_peers[d - 1]) for d in range(1, NX)]
    got(*sx)
    sends.extend(sx)
    srow = sg.at[core, ring, other]
    sy = [remote(srow, srow, sy_send.at[d], sy_recv.at[d], on_ring(ring, lax.rem(other + d, 8)))
          for d in range(1, 8)]
    at(2)
    got(*sy)
    sends.extend(sy)
    ra = rstep(0, 0)
    for c in ra:
        c().wait_send()
    del sends[-2:]
    rb = rstep(0, 1)
    share(0, 0)
    at(3)
    build(core, ring)
    def advance(t):
        T["ra"], old = None, T["ra"]
        got(*old)
        T["ra"] = rstep(t, 0)
        got(*T["rb"])
        T["rb"] = rstep(t, 1)
        share(2 * t - 1, -t)
        share(2 * t, t)
        at(3 + t)
        build(core, mod(ring - t, 8))
        build(core, mod(ring + t, 8))
        for slot in ((0,) if t == 1 else (2 * t - 3, 2 * t - 2)):
            got(cs[slot])
            build(1 - core, mod(other + (-(t - 1) if slot % 2 else t - 1), 8))

    T["ra"], T["rb"] = ra, rb
    advance(1)
    advance(2)
    got(x0[0, 1], x0[1, 0], *f0)

    @pl.loop(0, 8)
    def _(item):
        @pl.when(item == 1)
        def _():
            advance(3)
            got(*T["ra"], *T["rb"])
            share(7, 4)
            at(7)
            build(core, mod(ring + 4, 8))
            for slot, d in ((5, -3), (6, 3), (7, 4)):
                got(cs[slot])
                build(1 - core, mod(other + d, 8))

        @pl.when(item == 2)
        def _():
            at(8)
            got(T["x1"][0, 1], T["x1"][1, 0], *T["f1"])

        @pl.when(item == 4)
        def _():
            at(9)
            got(T["x2"][0, 1], T["x2"][1, 0], *T["f2"])

        @pl.when(item == 6)
        def _():
            at(10)
            got(T["x3"][0, 1], T["x3"][1, 0], *T["f3"])

        c = jnp.where(item < 2, 1 - item, lax.rem(item, 2))
        dy = jnp.where(item < 2, 0, jnp.where(item < 4, 3, jnp.where(item < 6, 1, 2)))
        process(c, lax.rem(yh + dy, NYH))

    for c in sends:
        (c() if callable(c) else c).wait_send()

    @pl.loop(0, NZ)
    def _(zz):
        for n in range(2):
            lanes = pl.ds(n * 128, 128)
            for lf in range(2):
                for lc in range(8):
                    turned[n, pl.ds(lf * 8 + lc, 32, stride=16), :] = acc[lf, pl.ds(zz * 256 + lc * 32, 32), lanes]
            both = turned[n].reshape(32, LB, 128) * (2.0 / F / W)
            out_ref[pl.ds(zz * 32, 32), :, lanes] = both.astype(jnp.bfloat16)


def on_device(spectra, source_block):
    dma = pltpu.SemaphoreType.DMA
    bf = jnp.bfloat16
    return pl.pallas_call(
        kernel,
        out_shape=jax.ShapeDtypeStruct((256, LB, 256), bf),
        in_specs=[
            pl.BlockSpec(memory_space=pltpu.SMEM),
            pl.BlockSpec(memory_space=pl.ANY),
        ],
        out_specs=pl.BlockSpec(memory_space=pltpu.VMEM),
        scratch_shapes=[
            pltpu.VMEM((2, FB, W, 256), bf),
            pltpu.VMEM((2, 2, W, 256), bf),
            pltpu.VMEM((4, NZ, 2, 16, 128), bf),
            pltpu.VMEM((4, NZ, 2, 16, 128), bf),
            pltpu.VMEM((NZ, 2, 16, 128), bf),
            pltpu.VMEM((NZ, 2, 16, 128), bf),
            pltpu.VMEM((NC, 8, 8, NX, 2, 16, 128), bf),
            pltpu.VMEM((NK, 512, 256), bf),
            pltpu.VMEM((1024, 256), bf),
            pltpu.VMEM((NK, 2, 8, 16, 128), bf),
            pltpu.VMEM((NK, 2, 8, 16, 128), bf),
            pltpu.VMEM((NC, NYH, 2048, 1024), bf),
            pltpu.VMEM((2, 2048, 256), jnp.float32),
            pltpu.VMEM((2, 512, 128), jnp.float32),
            dma((1,)),
            dma((2,)), dma((2,)),
            dma((4,)), dma((4,)),
            dma((8,)), dma((8,)),
            dma((4,)), dma((4,)),
            dma((8,)), dma((8,)),
            dma((2, 4, 2)), dma((2, 4, 2)),
            dma((8,)), dma((8,)),
            dma((2, 3)), dma((2, 3)),
            dma((4, 2, 3)), dma((4, 2, 3)),
        ],
        compiler_params=pltpu.CompilerParams(
            collective_id=0, has_side_effects=True, vmem_limit_bytes=56 * 2**20
        ),
        cost_estimate=pl.CostEstimate(flops=2 * 4096 * 8192 * 256, bytes_accessed=3 * 2**20, transcendentals=0),
    )(source_block, spectra)


def solution(mesh):
    in_specs = (P(None, "freq", None, "rx"), P())
    out_specs = P(None, "freq", "rx")
    return jax.shard_map(
        on_device, mesh=mesh, in_specs=in_specs, out_specs=out_specs, check_vma=False
    )
```

```python
import math

import jax
import jax.numpy as jnp
from jax import lax
from jax.experimental import pallas as pl
from jax.experimental.pallas import tpu as pltpu
from jax.sharding import PartitionSpec as P

F = 128
W = 32
LAGS = 256
NX, NYH, NYL, NZ, NC = 4, 4, 2, 8, 2
NK = NX * NYH
FB = F // NK
LB = LAGS // NK
MESH = pl.DeviceIdType.MESH


def mod(a, n):
    return lax.rem(a + n, n)


def kernel(owner_ref, spec_hbm, out_ref, spec_ref, halo, st_own, b2, sg, rg, rg1, cosb, sinb, lhs, acc, turned,
           spec_sem, halo_send, halo_recv, s1_send, s1_recv, sx_send, sx_recv,
           z_send, z_recv, c_send, c_recv, ry_send, ry_recv, rx_send, rx_recv):
    r = lax.axis_index("rx")
    k = lax.axis_index("freq")
    z = lax.div(r, 4)
    q = lax.rem(r, 4)
    yl = lax.div(q, 2)
    core = lax.rem(q, 2)
    yh = lax.div(k, 4)
    x = lax.rem(k, 4)

    def dev(z_, yl_, c_, yh_, x_):
        return (z_ * 4 + yl_ * 2 + c_, yh_ * 4 + x_)

    def remote(src, dst, send, recv, device):
        copy = pltpu.make_async_remote_copy(src, dst, send, recv, device_id=device, device_id_type=MESH)
        copy.start()
        return copy

    halo_peers = [(r, mod(k + 1, NK)), (r, mod(k - 1, NK))]
    y = yh * 2 + yl

    ring = jnp.where(core == 0, z, y)
    other = jnp.where(core == 0, y, z)
    place = other * NX + x

    def on_ring(a, b, x_):
        zz, yy = jnp.where(core == 0, a, b), jnp.where(core == 0, b, a)
        return dev(zz, lax.rem(yy, 2), core, lax.div(yy, 2), x_)

    ring_to = (on_ring(mod(ring + 1, 8), other, x), on_ring(mod(ring - 1, 8), other, x))

    def rx_peer(d):
        return (lax.rem(r + d, 32), k)

    def plane_peer(d):
        n = lax.rem(place + d, 32)
        return on_ring(ring, lax.div(n, NX), lax.rem(n, NX))

    y_to = (dev(z, yl, core, mod(yh + 1, NYH), x), dev(z, yl, core, mod(yh - 1, NYH), x))
    x_to = (dev(z, yl, core, yh, mod(x + 1, NX)), dev(z, yl, core, yh, mod(x - 1, NX)))
    sibling = dev(z, yl, 1 - core, yh, x)
    near = halo_peers + list(ring_to) + list(y_to)

    fetch = pltpu.make_async_copy(spec_hbm, spec_ref, spec_sem.at[0])
    fetch.start()
    barrier = pltpu.get_barrier_semaphore()
    for peer in near:
        pl.semaphore_signal(barrier, inc=1, device_id=peer, device_id_type=MESH)

    @pl.loop(1, 32)
    def _(d):
        pl.semaphore_signal(barrier, inc=1, device_id=rx_peer(d), device_id_type=MESH)
        pl.semaphore_signal(barrier, inc=1, device_id=plane_peer(d), device_id_type=MESH)

    pl.semaphore_wait(barrier, len(near) + 62)

    up, down = halo_peers
    h0 = remote(spec_hbm.at[:, FB - 1], halo.at[0], halo_send.at[0], halo_recv.at[0], up)
    h1 = remote(spec_hbm.at[:, 0], halo.at[1], halo_send.at[1], halo_recv.at[1], down)

    lane = lax.broadcasted_iota(jnp.int32, (8, FB * W), 1)
    lag = lax.broadcasted_iota(jnp.int32, (8, FB * W), 0) + k * LB

    @pl.loop(0, NK)
    def _(kk):
        bins = kk * FB + lax.shift_right_logical(lane, 5)
        angle = jnp.bitwise_and(bins * lag, LAGS - 1).astype(jnp.float32) * (2.0 * math.pi / LAGS)
        for table, values in ((cosb, jnp.cos(angle)), (sinb, jnp.sin(angle))):
            for c in range(2):
                for lc in range(8):
                    line = values[lc:lc + 1, c * 128:(c + 1) * 128]
                    table[kk, c, lc] = jnp.broadcast_to(line, (16, 128)).astype(jnp.bfloat16)

    fetch.wait()
    acc[...] = jnp.zeros_like(acc)
    h0.wait()
    h1.wait()

    def magnitude(a, b):
        return jnp.sqrt(a * a + b * b)

    lower = halo[0].astype(jnp.float32)
    upper = halo[1].astype(jnp.float32)
    m_low = jnp.where(k == 0, 0.0, magnitude(lower[0], lower[1]))
    m_high = jnp.where(k == NK - 1, 0.0, magnitude(upper[0], upper[1]))

    def raw(p, f):
        return spec_ref[p, f].astype(jnp.float32)

    mags = [m_low] + [magnitude(raw(0, f), raw(1, f)) for f in range(FB)] + [m_high]
    for f in range(FB):
        divisor = jnp.maximum((mags[f] + mags[f + 1] + mags[f + 2]) / 3.0, 0.5)
        for p in range(2):
            rg[k, pl.ds(f // 4 * 256 + p * 128 + f % 4 * W, W), :] = (raw(p, f) / divisor).astype(jnp.bfloat16)

    half = (pl.ds(0, 256), pl.ds(256, 256))
    sends = []

    def block_of(dyh, dx):
        return mod(yh + dyh, NYH) * NX + mod(x + dx, NX)

    def launch(make):
        make().start()
        sends.append(make)
        return make

    def ry(way, slot, block, h):
        def make():
            view = rg.at[block_of(*block), half[h]]
            return pltpu.make_async_remote_copy(view, view, ry_send.at[way, slot], ry_recv.at[way, slot],
                                                device_id=y_to[way], device_id_type=MESH)

        return launch(make)

    def rx(row, way, slot, block, h):
        def make():
            view = rg.at[block_of(*block), half[h]]
            return pltpu.make_async_remote_copy(view, view, rx_send.at[row, way, slot], rx_recv.at[row, way, slot],
                                                device_id=x_to[way], device_id_type=MESH)

        return launch(make)

    def got(*copies):
        for c in copies:
            (c() if callable(c) else c).wait_recv()

    def xsend(row, block, h):
        return {(0, h): rx(row, 0, h, block, h), (1, h): rx(row, 1, h, block, h)}

    def rpart(t, u, way):
        def make():
            view = sg.at[core, mod(ring - t, 8) if way == 0 else mod(ring + t, 8), pl.ds(u * 4, 4)]
            return pltpu.make_async_remote_copy(view, view, z_send.at[way, t, u], z_recv.at[way, t, u],
                                                device_id=ring_to[way], device_id_type=MESH)

        return launch(make)

    def rstep(t, u):
        return [rpart(t, u, way) for way in range(2) if t < 3 or way == u]

    cs = []

    def share(slot, a):
        def make():
            view = sg.at[core, mod(ring + a, 8)]
            return pltpu.make_async_remote_copy(view, view, c_send.at[slot], c_recv.at[slot],
                                                device_id=sibling, device_id_type=MESH)

        cs.append(launch(make))

    def build(c, a):
        @pl.loop(0, 8)
        def _(b):
            zz, yy = jnp.where(c == 0, a, b), jnp.where(c == 0, b, a)
            row, yl_ = lax.div(yy, 2), lax.rem(yy, 2)
            for xx in range(NX):
                kk = row * NX + xx
                s0, s1_ = sg[c, a, b, xx, 0], sg[c, a, b, xx, 1]
                for lc in range(8):
                    co, si = cosb[kk, c, lc], sinb[kk, c, lc]
                    rows = pl.ds(pl.multiple_of(zz * 256 + lc * 32 + yl_ * 16, 16), 16)
                    lhs[c, row, rows, pl.ds(xx * 256, 128)] = co * s0 + si * s1_
                    lhs[c, row, rows, pl.ds(xx * 256 + 128, 128)] = co * s1_ - si * s0

    def process(c, row):
        for xx in range(NX):
            kk = row * NX + xx
            for g in range(4):
                angles = [2.0 * math.pi / 32 * (xx * FB + m * 4 + g) for m in range(2)]
                cr = jnp.where(c == 0, math.cos(angles[0]), math.cos(angles[1]))
                ci = jnp.where(c == 0, math.sin(angles[0]), math.sin(angles[1]))
                a = rg[kk, pl.ds(pl.multiple_of(c * 256 + g * W, W), W), :].astype(jnp.float32)
                b = rg[kk, pl.ds(pl.multiple_of(c * 256 + 128 + g * W, W), W), :].astype(jnp.float32)
                rg1[pl.ds(xx * 256 + g * W, W), :] = (a * cr - b * ci).astype(jnp.bfloat16)
                rg1[pl.ds(xx * 256 + 128 + g * W, W), :] = (b * cr + a * ci).astype(jnp.bfloat16)
        left = lhs[c, row]
        right = rg[pl.ds(row * NX, NX), pl.ds(pl.multiple_of(c * 256, 256), 256), :].reshape(1024, 256)
        acc[0] += jnp.dot(left, right, preferred_element_type=jnp.float32)
        acc[1] += jnp.dot(left, rg1[...], preferred_element_type=jnp.float32)

    for p in range(2):
        for c in range(2):
            t = rg[k, pl.ds(c * 256 + p * 128, 128), :].astype(jnp.float32).T.astype(jnp.bfloat16)
            t = t.reshape(NZ, 2, 16, 128)
            for yl_ in range(2):
                st_own[:, yl_ * 2 + c, p] = t[:, yl_]

    def exchange(d):
        j = lax.rem(r + d, 32)
        return pltpu.make_async_remote_copy(st_own.at[lax.div(j, 4), lax.rem(j, 4)], b2.at[r], s1_send.at[d],
                                            s1_recv.at[d], device_id=rx_peer(d), device_id_type=MESH)

    def spread(d):
        view = sg.at[core, ring, other, x]
        return pltpu.make_async_remote_copy(view, view, sx_send.at[d], sx_recv.at[d],
                                            device_id=plane_peer(d), device_id_type=MESH)

    @pl.loop(1, 32)
    def _(d):
        exchange(d).start()

    T = {}
    plan = dict(y0=1, y1=3, g0=2, y2=5, g1=4, fa=4, fb=5, g2=7, f3=8)

    def at(point):
        for name, step in events:
            if plan[name] == point:
                step()

    def y0():
        T["y0"] = (ry(0, 0, (0, 0), 0), ry(1, 1, (0, 0), 1))

    def y1():
        T["y1"] = (ry(0, 1, (0, 0), 1), ry(1, 0, (0, 0), 0))

    def g0():
        got(*T["y0"])
        T["x1"] = xsend(1, (-1, 0), 0)
        T["x2"] = xsend(2, (1, 0), 1)

    def y2():
        T["y2"] = (ry(0, 2, (-1, 0), 0), ry(1, 2, (1, 0), 1))

    def g1():
        got(*T["y1"])
        T["x1"].update(xsend(1, (-1, 0), 1))
        T["x2"].update(xsend(2, (1, 0), 0))

    def fa():
        got(T["x1"][0, 0], T["x2"][1, 1])
        T["f1"] = [rx(1, 0, 2, (-1, -1), 0)]
        T["f2"] = [rx(2, 1, 2, (1, 1), 1)]

    def fb():
        got(T["x1"][1, 1], T["x2"][0, 0])
        T["f1"].append(rx(1, 1, 2, (-1, 1), 1))
        T["f2"].append(rx(2, 0, 2, (1, -1), 0))

    def g2():
        got(*T["y2"])
        T["x3"] = xsend(3, (2, 0), 0)
        T["x3"].update(xsend(3, (2, 0), 1))

    def f3():
        got(T["x3"][0, 0], T["x3"][1, 1])
        T["f3"] = [rx(3, 0, 2, (2, -1), 0), rx(3, 1, 2, (2, 1), 1)]

    events = [("y0", y0), ("y1", y1), ("g0", g0), ("y2", y2), ("g1", g1), ("fa", fa), ("fb", fb), ("g2", g2), ("f3", f3)]

    at(0)
    x0 = {(0, 0): rx(0, 0, 0, (0, 0), 0), (1, 1): rx(0, 1, 1, (0, 0), 1)}
    x0[0, 1] = rx(0, 0, 1, (0, 0), 1)
    x0[1, 0] = rx(0, 1, 0, (0, 0), 0)
    b2[r] = st_own[z, q]
    owner = owner_ref[0]
    got(x0[0, 0], x0[1, 1])
    f0 = (rx(0, 0, 2, (0, -1), 0), rx(0, 1, 2, (0, 1), 1))

    @pl.loop(1, 32)
    def _(d):
        exchange(d).wait_recv()

    sg[core, ring, other, x] = b2[owner]

    @pl.loop(1, 32)
    def _(d):
        spread(d).start()

    at(1)
    at(2)

    @pl.loop(1, 32)
    def _(d):
        spread(d).wait_recv()

    ra = rstep(0, 0)
    for c in ra:
        c().wait_send()
    del sends[-2:]
    rb = rstep(0, 1)
    share(0, 0)
    at(3)
    build(core, ring)
    def advance(t):
        T["ra"], old = None, T["ra"]
        got(*old)
        T["ra"] = rstep(t, 0)
        got(*T["rb"])
        T["rb"] = rstep(t, 1)
        share(2 * t - 1, -t)
        share(2 * t, t)
        at(3 + t)
        build(core, mod(ring - t, 8))
        build(core, mod(ring + t, 8))
        for slot in ((0,) if t == 1 else (2 * t - 3, 2 * t - 2)):
            got(cs[slot])
            build(1 - core, mod(other + (-(t - 1) if slot % 2 else t - 1), 8))

    T["ra"], T["rb"] = ra, rb
    advance(1)
    advance(2)
    got(x0[0, 1], x0[1, 0], *f0)

    @pl.loop(0, 8)
    def _(item):
        @pl.when(item == 1)
        def _():
            advance(3)
            got(*T["ra"], *T["rb"])
            share(7, 4)
            at(7)
            build(core, mod(ring + 4, 8))
            for slot, d in ((5, -3), (6, 3), (7, 4)):
                got(cs[slot])
                build(1 - core, mod(other + d, 8))

        @pl.when(item == 2)
        def _():
            at(8)
            got(T["x1"][0, 1], T["x1"][1, 0], *T["f1"])

        @pl.when(item == 4)
        def _():
            at(9)
            got(T["x2"][0, 1], T["x2"][1, 0], *T["f2"])

        @pl.when(item == 6)
        def _():
            at(10)
            got(T["x3"][0, 1], T["x3"][1, 0], *T["f3"])

        c = jnp.where(item < 2, 1 - item, lax.rem(item, 2))
        dy = jnp.where(item < 2, 0, jnp.where(item < 4, 3, jnp.where(item < 6, 1, 2)))
        process(c, lax.rem(yh + dy, NYH))

    @pl.loop(1, 32)
    def _(d):
        exchange(d).wait_send()
        spread(d).wait_send()

    for c in sends:
        (c() if callable(c) else c).wait_send()

    @pl.loop(0, NZ)
    def _(zz):
        for n in range(2):
            lanes = pl.ds(n * 128, 128)
            for lf in range(2):
                for lc in range(8):
                    turned[n, pl.ds(lf * 8 + lc, 32, stride=16), :] = acc[lf, pl.ds(zz * 256 + lc * 32, 32), lanes]
            both = turned[n].reshape(32, LB, 128) * (2.0 / F / W)
            out_ref[pl.ds(zz * 32, 32), :, lanes] = both.astype(jnp.bfloat16)


def on_device(spectra, source_block):
    dma = pltpu.SemaphoreType.DMA
    bf = jnp.bfloat16
    return pl.pallas_call(
        kernel,
        out_shape=jax.ShapeDtypeStruct((256, LB, 256), bf),
        in_specs=[
            pl.BlockSpec(memory_space=pltpu.SMEM),
            pl.BlockSpec(memory_space=pl.ANY),
        ],
        out_specs=pl.BlockSpec(memory_space=pltpu.VMEM),
        scratch_shapes=[
            pltpu.VMEM((2, FB, W, 256), bf),
            pltpu.VMEM((2, 2, W, 256), bf),
            pltpu.VMEM((NZ, 4, 2, 16, 128), bf),
            pltpu.VMEM((32, 2, 16, 128), bf),
            pltpu.VMEM((NC, 8, 8, NX, 2, 16, 128), bf),
            pltpu.VMEM((NK, 512, 256), bf),
            pltpu.VMEM((1024, 256), bf),
            pltpu.VMEM((NK, 2, 8, 16, 128), bf),
            pltpu.VMEM((NK, 2, 8, 16, 128), bf),
            pltpu.VMEM((NC, NYH, 2048, 1024), bf),
            pltpu.VMEM((2, 2048, 256), jnp.float32),
            pltpu.VMEM((2, 512, 128), jnp.float32),
            dma((1,)),
            dma((2,)), dma((2,)),
            dma((32,)), dma((32,)),
            dma((32,)), dma((32,)),
            dma((2, 4, 2)), dma((2, 4, 2)),
            dma((8,)), dma((8,)),
            dma((2, 3)), dma((2, 3)),
            dma((4, 2, 3)), dma((4, 2, 3)),
        ],
        compiler_params=pltpu.CompilerParams(
            collective_id=0, has_side_effects=True, vmem_limit_bytes=56 * 2**20
        ),
        cost_estimate=pl.CostEstimate(flops=2 * 4096 * 8192 * 256, bytes_accessed=3 * 2**20, transcendentals=0),
    )(source_block, spectra)


def solution(mesh):
    in_specs = (P(None, "freq", None, "rx"), P())
    out_specs = P(None, "freq", "rx")
    return jax.shard_map(
        on_device, mesh=mesh, in_specs=in_specs, out_specs=out_specs, check_vma=False
    )
```
